512 devices in a mesh: row: 16 (over x, y_lo, core), col: 32 (over y_hi, z).
Axes of the slice: x: 4, y: 4 (y_hi: 2, y_lo: 2; y = y_hi * 2 + y_lo), z: 16, core: 2. Of those that a mesh axis runs over, the one named last changes fastest.
Arguments:
- features: bfloat16 [49152, 128], P(('col', 'row')), may hold values from -6 to 6
- weight: bfloat16 [128, 256], replicated, may hold values from -0.5 to 0.5
- bias: float32 [256], replicated, may hold values from -3 to 3
- tile_values: bfloat16 [16, 32, 128, 128, 128], P('row', 'col'), may hold values from -0.0390625 to 0.0390625
- tile_rows: int32 [16, 32, 128], P('row', 'col'), may hold values from 0 to 23
- tile_cols: int32 [16, 32, 128], P('row', 'col'), may hold values from 0 to 11
- tile_count: int32 [16, 32], P('row', 'col'), may hold values from 16 to 128, as said below
Outputs:
- hidden: bfloat16 [49152, 256], P(('row', 'col'))
The draws below stay inside these ranges and needn't reach their ends.
Inputs may be any that keep to these rules, and one draw needn't show every extreme that they name: `tile_count`: within one row block and column block the 128 slots name distinct tile positions. Some block's count equals 128 in every draw.
All inputs are finite; a program needn't handle non-finite values.
Results may differ from the reference program's by a relative error of at most 0.0019.
Values may be sent and summed in bfloat16 or wider, within the bound.
No kernel may reach another device: no remote copies, remote signals or barrier semaphores. Data moves between devices by JAX's collectives and lax.ppermute only.
A program may use at most 64 MiB of HBM per device.

```python
import jax
import jax.numpy as jnp
from jax import lax

TILE = 128
F_IN = 128
F_OUT = 256
BC = 12
CAP = 128
BR = 24
NODES = 49152
N_ROW = 16
N_COL = 32


def tile_positions(key):
    base_key = jax.random.fold_in(key, 7)
    device_keys = jax.random.split(base_key, N_ROW * N_COL)
    shuffled = jax.vmap(lambda device_key: jax.random.permutation(device_key, BR * BC)[:CAP])(device_keys)
    return shuffled.reshape(N_ROW, N_COL, CAP).astype(jnp.int32)


def draw_tile_rows(key, part):
    return tile_positions(key) // BC


def draw_tile_cols(key, part):
    return tile_positions(key) % BC


def draw_tile_count(key, part):
    first_key = jax.random.fold_in(key, 11)
    second_key = jax.random.fold_in(key, 13)
    tile_counts = jax.random.randint(first_key, (N_ROW * N_COL,), max(1, CAP // 8), CAP + 1)
    chosen_block = jax.random.randint(second_key, (), 0, N_ROW * N_COL)
    tile_counts = tile_counts.at[chosen_block].set(CAP)
    return tile_counts.reshape(N_ROW, N_COL).astype(jnp.int32)


def steps_of(key, dims, cuts, low, largest):
    level = 1.0
    for axis_at, blocks in cuts:
        steps = jax.random.uniform(jax.random.fold_in(jax.random.fold_in(key, 6), axis_at), (blocks,), jnp.float32, low / len(cuts), largest / len(cuts))
        level = level * jnp.repeat(jnp.exp(steps), dims[axis_at] // blocks).reshape((-1,) + (1,) * (len(dims) - 1 - axis_at))
    return level


def scatter_about(own_key, shape, deviation, reach, cuts=(), kind=jnp.bfloat16):
    array = jax.random.normal(own_key, shape, jnp.float32) * deviation
    if len(cuts) > 0:
        array = steps_of(own_key, shape, cuts, -0.22, 0.18) * array
    return jnp.clip(array, min=-reach, max=reach).astype(kind)


def setup_inputs(seed: int = 0) -> dict:
    arg_keys = jax.random.split(jax.random.key(seed), 8)
    return {
        "features": scatter_about(arg_keys[0], (NODES, F_IN), 1.0, 6.0, ((0, 512),)),
        "weight": scatter_about(arg_keys[1], (F_IN, F_OUT), F_IN ** -0.5, 0.5),
        "bias": scatter_about(arg_keys[2], (F_OUT,), 0.5, 3.0, (), jnp.float32),
        "tile_values": scatter_about(arg_keys[3], (N_ROW, N_COL, CAP, TILE, TILE), (TILE * CAP * N_COL // BR) ** -0.5, 0.0390625, ((0, 16), (1, 32))),
        "tile_rows": draw_tile_rows(jax.random.fold_in(arg_keys[7], 71), 0),
        "tile_cols": draw_tile_cols(jax.random.fold_in(arg_keys[7], 71), 0),
        "tile_count": draw_tile_count(jax.random.fold_in(arg_keys[7], 71), 0),
    }


def reference(features, weight, bias, tile_values, tile_rows, tile_cols, tile_count):
    feature_table = features.astype(jnp.float32).reshape(N_COL, BC, TILE, F_IN)
    slot_index = jnp.arange(CAP, dtype=jnp.int32)
    row_index = jnp.arange(BR, dtype=jnp.int32)

    def one_row(row_block):
        def one_col(running, col_block):
            values = tile_values[row_block, col_block].astype(jnp.float32)
            row_ids = tile_rows[row_block, col_block]
            col_ids = tile_cols[row_block, col_block]
            chosen = feature_table[col_block][col_ids]
            products = jnp.einsum("tij,tjf->tif", values, chosen, precision=lax.Precision.HIGHEST)
            alive_mask = (slot_index < tile_count[row_block, col_block]).astype(jnp.float32)
            selector = (row_ids[:, None] == row_index[None, :]).astype(jnp.float32) * alive_mask[:, None]
            running = running + jnp.einsum("tr,tif->rif", selector, products, precision=lax.Precision.HIGHEST)
            return running, None

        running, unused = lax.scan(one_col, jnp.zeros((BR, TILE, F_IN), jnp.float32), jnp.arange(N_COL, dtype=jnp.int32))
        return running.reshape(BR * TILE, F_IN)

    aggregated = lax.map(one_row, jnp.arange(N_ROW, dtype=jnp.int32)).reshape(N_ROW * BR * TILE, F_IN)
    output = jnp.dot(aggregated, weight.astype(jnp.float32), precision=lax.Precision.HIGHEST) + bias
    return jax.nn.relu(output).astype(jnp.bfloat16)
```

```python
import functools

import jax
import jax.numpy as jnp
from jax import lax
from jax.experimental import pallas as pl
from jax.experimental.pallas import tpu as pltpu
from jax.sharding import PartitionSpec as P

LEVELS = 12
STEP = 10
EXTRA = 8


def level_of(peak, base):
    level = jnp.zeros(peak.shape, jnp.float32)
    for k in range(1, LEVELS + 1):
        level = level + jnp.where(peak < 2.0 ** (15 - base - STEP * k), 1.0, 0.0)
    return level


def power(level, sign):
    value = jnp.ones(level.shape, jnp.float32)
    for k in range(1, LEVELS + 1):
        value = value * jnp.where(level >= k, 2.0 ** (sign * STEP), 1.0)
    return value


def spread_kernel(tile, rows_ref, cols_ref, count_ref, tiles_ref, dense_ref, sems):
    used = count_ref[0]
    lines = 2 * tile

    def clear(i, carry):
        span = pl.ds(pl.multiple_of(i * lines, lines), lines)
        dense_ref[span, :] = jnp.zeros((lines, dense_ref.shape[1]), dense_ref.dtype)
        return carry

    lax.fori_loop(0, dense_ref.shape[0] // lines, clear, 0)

    def move(s):
        row = pl.multiple_of(rows_ref[s] * tile, tile)
        col = pl.multiple_of(cols_ref[s] * tile, tile)
        return pltpu.make_async_copy(
            tiles_ref.at[s], dense_ref.at[pl.ds(row, tile), pl.ds(col, tile)], sems.at[s]
        )

    def start(s, carry):
        move(s).start()
        return carry

    def wait(s, carry):
        move(s).wait()
        return carry

    lax.fori_loop(0, used, start, 0)
    lax.fori_loop(0, used, wait, 0)


def product_kernel(parts, base, dense_ref, x_ref, out_ref, held, sems):
    ways, depth, share = parts
    near = ways // 2
    per = ways * depth // sems.shape[0]

    def fetch(g):
        span = pl.ds(g * per * share, per * share)
        return pltpu.make_async_copy(dense_ref.at[span, :], held.at[span, :], sems.at[g])

    for g in range(sems.shape[0]):
        fetch(g).start()
    for d in range(ways * depth):
        if d % per == 0:
            fetch(d // per).wait()
        way = (d // (near * depth)) * near + d % near
        place = (d % (near * depth)) // near
        value = jnp.dot(held[d * share : (d + 1) * share, :], x_ref[...], preferred_element_type=jnp.float32)
        level = level_of(jnp.max(jnp.abs(value), axis=0, keepdims=True), base)
        out_ref[way, place * share : (place + 1) * share, :] = value * (power(level, 1) * 2.0**base)
        out_ref[way, depth * share + place : depth * share + place + 1, :] = level


def shards(mesh, features, weight, bias, tile_values, tile_rows, tile_cols, tile_count):
    tiles = tile_values[0, 0]
    slots, tile, _ = tiles.shape
    width = features.shape[1]
    n_row, n_col = mesh.shape["row"], mesh.shape["col"]
    share = features.shape[0]
    total_rows = share * n_col
    half = n_col // 2
    near = 2
    ways = 2 * near
    depth = n_col // ways

    spread = jnp.broadcast_to(features[None], (n_row,) + features.shape)
    gathered = lax.all_to_all(spread, "row", 0, 0).reshape(n_row * features.shape[0], width)

    dense = pl.pallas_call(
        functools.partial(spread_kernel, tile),
        out_shape=jax.ShapeDtypeStruct((total_rows, n_row * features.shape[0]), tiles.dtype),
        in_specs=[pl.BlockSpec(memory_space=pltpu.SMEM)] * 3 + [pl.BlockSpec(memory_space=pltpu.HBM)],
        out_specs=pl.BlockSpec(memory_space=pltpu.VMEM),
        scratch_shapes=[pltpu.SemaphoreType.DMA((slots,))],
        compiler_params=pltpu.CompilerParams(vmem_limit_bytes=60 * 2**20),
        cost_estimate=pl.CostEstimate(flops=0, bytes_accessed=6 * slots * tile * tile, transcendentals=0),
    )(tile_rows[0, 0], tile_cols[0, 0], tile_count[0], tiles)

    base = 7
    message = pl.pallas_call(
        functools.partial(product_kernel, (ways, depth, share), base),
        out_shape=jax.ShapeDtypeStruct((ways, depth * share + depth, width), jnp.float32),
        in_specs=[pl.BlockSpec(memory_space=pltpu.HBM), pl.BlockSpec(memory_space=pltpu.VMEM)],
        out_specs=pl.BlockSpec(memory_space=pltpu.VMEM),
        scratch_shapes=[pltpu.VMEM(dense.shape, dense.dtype), pltpu.SemaphoreType.DMA((8,))],
        compiler_params=pltpu.CompilerParams(vmem_limit_bytes=50 * 2**20),
    )(dense, gathered)

    pairs = [[h * half + p * near + q for h in range(2) for q in range(near)] for p in range(depth)]
    came = lax.all_to_all(message.astype(jnp.float16), "col", 0, 0, axis_index_groups=pairs).astype(jnp.float32)
    spot = depth * share
    unit = (power(came[:, spot:], -1) * 2.0**-base)[:, :, None]
    blocks = jnp.sum(came[:, :spot].reshape(ways, depth, share, width) * unit, axis=0)

    base = 5
    level = level_of(jnp.max(jnp.abs(blocks), axis=1, keepdims=True), base)
    scaled = blocks * (power(level, 1) * 2.0**base)
    message = jnp.concatenate([scaled, jnp.broadcast_to(level, (depth, EXTRA, width))], axis=1).astype(jnp.float16)
    rest = [[h * half + p * near + q for p in range(depth)] for h in range(2) for q in range(near)]
    came = lax.all_to_all(message, "col", 0, 0, axis_index_groups=rest).astype(jnp.float32)
    summed = jnp.sum(came[:, :share] * (power(came[:, share : share + 1], -1) * 2.0**-base), axis=0)

    output = jnp.dot(summed, weight.astype(jnp.float32), precision=lax.Precision.HIGHEST) + bias
    return jax.nn.relu(output).astype(jnp.bfloat16)


def solution(mesh):
    in_specs = (
        P(("col", "row"), None),
        P(),
        P(),
        P("row", "col", None, None, None),
        P("row", "col", None),
        P("row", "col", None),
        P("row", "col"),
    )
    out_specs = P(("row", "col"), None)
    return jax.shard_map(
        functools.partial(shards, mesh), mesh=mesh, in_specs=in_specs, out_specs=out_specs, check_vma=False
    )
```

```python
import functools

import jax
import jax.numpy as jnp
from jax import lax
from jax.experimental import pallas as pl
from jax.experimental.pallas import tpu as pltpu
from jax.sharding import PartitionSpec as P

LEVELS = 6
STEP = 16
ROOT = 1024.0


def level_of(peak, base):
    level = jnp.zeros(peak.shape, jnp.float32)
    for k in range(1, LEVELS + 1):
        level = level + jnp.where(peak < 2.0 ** (15 - base - STEP * k), 1.0, 0.0)
    return level


def power(level, sign):
    value = jnp.ones(level.shape, jnp.float32)
    for k in range(1, LEVELS + 1):
        value = value * jnp.where(level >= k, 2.0 ** (sign * STEP), 1.0)
    return value


def product_kernel(parts, base, spot_ref, tiles_ref, x_ref, out_ref, place_ref, held, sems):
    ways, depth, share, row_tiles, col_tiles = parts
    slots, tile, _ = held.shape
    chunks = sems.shape[0]
    per = slots // chunks

    def fetch(g):
        span = pl.ds(g * per, per)
        return pltpu.make_async_copy(tiles_ref.at[0, 0, span], held.at[span], sems.at[g])

    for g in range(chunks):
        fetch(g).start()
    near = ways // 2
    spots = row_tiles * col_tiles

    for p in range(spots):
        place_ref[p] = slots
    for s in range(slots):
        place_ref[spot_ref[s]] = s

    for g in range(chunks):
        fetch(g).wait()

    def piece(p, lo, hi):
        slot = place_ref[p]
        rows = held[jnp.minimum(slot, slots - 1), lo:hi, :]
        return jnp.where(slot < slots, rows, jnp.zeros_like(rows))

    for d in range(ways * depth):
        way = (d // (near * depth)) * near + d % near
        at = (d % (near * depth)) // near
        value = jnp.zeros((share, x_ref.shape[1]), jnp.float32)
        for j in range(0, col_tiles, 2):
            strips = []
            row = d * share
            while row < (d + 1) * share:
                r, lo = row // tile, row % tile
                hi = min(tile, lo + (d + 1) * share - row)
                strips.append(
                    jnp.concatenate([piece(r * col_tiles + j + k, lo, hi) for k in range(2)], axis=1)
                )
                row += hi - lo
            value = value + jnp.dot(
                jnp.concatenate(strips, axis=0),
                x_ref[j * tile : (j + 2) * tile, :],
                preferred_element_type=jnp.float32,
            )
        level = level_of(jnp.max(jnp.abs(value), axis=0, keepdims=True), base)
        out_ref[way, at * share : (at + 1) * share, :] = value * (power(level, 1) * 2.0**base)
        out_ref[way, depth * share + at : depth * share + at + 1, :] = level


def shards(mesh, features, weight, bias, tile_values, tile_rows, tile_cols, tile_count):
    tile = tile_values.shape[3]
    width = features.shape[1]
    n_row, n_col = mesh.shape["row"], mesh.shape["col"]
    share = features.shape[0]
    total_rows = share * n_col
    half = n_col // 2
    near = 2
    ways = 2 * near
    depth = n_col // ways

    spread = jnp.broadcast_to(features[None], (n_row,) + features.shape)
    row_tiles, col_tiles = total_rows // tile, n_row * share // tile
    used = jnp.arange(tile_rows.shape[2], dtype=jnp.int32) < tile_count[0, 0]
    spots = jnp.where(used, tile_rows[0, 0] * col_tiles + tile_cols[0, 0], row_tiles * col_tiles)
    spread, spots = lax.optimization_barrier((spread, spots))
    gathered = lax.all_to_all(spread, "row", 0, 0).reshape(n_row * features.shape[0], width)

    base = 7
    message = pl.pallas_call(
        functools.partial(product_kernel, (ways, depth, share, row_tiles, col_tiles), base),
        out_shape=jax.ShapeDtypeStruct((ways, depth * share + depth, width), jnp.float32),
        in_specs=[pl.BlockSpec(memory_space=m) for m in (pltpu.SMEM, pltpu.HBM, pltpu.VMEM)],
        out_specs=pl.BlockSpec(memory_space=pltpu.VMEM),
        scratch_shapes=[
            pltpu.SMEM((row_tiles * col_tiles + 8,), jnp.int32),
            pltpu.VMEM(tile_values.shape[2:], tile_values.dtype),
            pltpu.SemaphoreType.DMA((8,)),
        ],
        compiler_params=pltpu.CompilerParams(vmem_limit_bytes=50 * 2**20),
    )(spots, tile_values, gathered)

    pairs = [[h * half + p * near + q for h in range(2) for q in range(near)] for p in range(depth)]
    came = lax.all_to_all(message.astype(jnp.float16), "col", 0, 0, axis_index_groups=pairs).astype(jnp.float32)
    spot = depth * share
    unit = (power(came[:, spot:], -1) * 2.0**-base)[:, :, None]
    blocks = jnp.sum(came[:, :spot].reshape(ways, depth, share, width) * unit, axis=0)

    rest = [[h * half + p * near + q for p in range(depth)] for h in range(2) for q in range(near)]
    message = (jnp.where(blocks < 0, -ROOT, ROOT) * jnp.sqrt(jnp.abs(blocks))).astype(jnp.float16)
    came = lax.all_to_all(message, "col", 0, 0, axis_index_groups=rest).astype(jnp.float32)
    summed = jnp.sum(came * jnp.abs(came), axis=0) * ROOT**-2

    output = jnp.dot(summed, weight.astype(jnp.float32), precision=lax.Precision.HIGHEST) + bias
    return jax.nn.relu(output).astype(jnp.bfloat16)


def solution(mesh):
    in_specs = (
        P(("col", "row"), None),
        P(),
        P(),
        P("row", "col", None, None, None),
        P("row", "col", None),
        P("row", "col", None),
        P("row", "col"),
    )
    out_specs = P(("row", "col"), None)
    return jax.shard_map(
        functools.partial(shards, mesh), mesh=mesh, in_specs=in_specs, out_specs=out_specs, check_vma=False
    )
```

```python
import functools

import jax
import jax.numpy as jnp
from jax import lax
from jax.experimental import pallas as pl
from jax.experimental.pallas import tpu as pltpu
from jax.sharding import PartitionSpec as P

LEVELS = 6
STEP = 16
ROOT = 1024.0


def level_of(peak, base):
    level = jnp.zeros(peak.shape, jnp.float32)
    for k in range(1, LEVELS + 1):
        level = level + jnp.where(peak < 2.0 ** (15 - base - STEP * k), 1.0, 0.0)
    return level


def power(level, sign):
    value = jnp.ones(level.shape, jnp.float32)
    for k in range(1, LEVELS + 1):
        value = value * jnp.where(level >= k, 2.0 ** (sign * STEP), 1.0)
    return value


def spread_kernel(features_ref, tiles_ref, spread_ref):
    for k in range(spread_ref.shape[0]):
        spread_ref[k] = features_ref[...]


def product_kernel(parts, base, spot_ref, tiles_ref, x_ref, out_ref, place_ref):
    ways, depth, share, row_tiles, col_tiles = parts
    _, _, slots, tile, _ = tiles_ref.shape
    near = ways // 2
    for p in range(row_tiles * col_tiles):
        place_ref[p] = slots
    for s in range(slots):
        place_ref[spot_ref[0, s]] = s

    def piece(p, lo, hi):
        slot = place_ref[p]
        rows = tiles_ref[0, 0, jnp.minimum(slot, slots - 1), lo:hi, :]
        return jnp.where(slot < slots, rows, jnp.zeros_like(rows))

    for d in range(ways * depth):
        way = (d // (near * depth)) * near + d % near
        at = (d % (near * depth)) // near
        value = jnp.zeros((share, x_ref.shape[1]), jnp.float32)
        for j in range(0, col_tiles, 2):
            strips = []
            row = d * share
            while row < (d + 1) * share:
                r, lo = row // tile, row % tile
                hi = min(tile, lo + (d + 1) * share - row)
                strips.append(
                    jnp.concatenate([piece(r * col_tiles + j + k, lo, hi) for k in range(2)], axis=1)
                )
                row += hi - lo
            value = value + jnp.dot(
                jnp.concatenate(strips, axis=0),
                x_ref[j * tile : (j + 2) * tile, :],
                preferred_element_type=jnp.float32,
            )
        level = level_of(jnp.max(jnp.abs(value), axis=0, keepdims=True), base)
        out_ref[way, at * share : (at + 1) * share, :] = value * (power(level, 1) * 2.0**base)
        out_ref[way, depth * share + at : depth * share + at + 1, :] = level


def shards(mesh, features, weight, bias, tile_values, tile_rows, tile_cols, tile_count):
    tile = tile_values.shape[3]
    width = features.shape[1]
    n_row, n_col = mesh.shape["row"], mesh.shape["col"]
    share = features.shape[0]
    total_rows = share * n_col
    half = n_col // 2
    near = 2
    ways = 2 * near
    depth = n_col // ways

    row_tiles, col_tiles = total_rows // tile, n_row * share // tile
    used = jnp.arange(tile_rows.shape[2], dtype=jnp.int32) < tile_count[0, 0]
    spots = jnp.where(used, tile_rows[0] * col_tiles + tile_cols[0], row_tiles * col_tiles)
    slots = tile_rows.shape[2]
    smem, vmem = pl.BlockSpec(memory_space=pltpu.SMEM), pl.BlockSpec(memory_space=pltpu.VMEM)
    spread = pl.pallas_call(
        spread_kernel,
        out_shape=jax.ShapeDtypeStruct((n_row,) + features.shape, features.dtype),
        in_specs=[vmem, pl.BlockSpec(memory_space=pltpu.HBM)],
        out_specs=vmem,
        compiler_params=pltpu.CompilerParams(vmem_limit_bytes=50 * 2**20),
    )(features, tile_values)
    spread, spots = lax.optimization_barrier((spread, spots))
    gathered = lax.all_to_all(spread, "row", 0, 0).reshape(n_row * features.shape[0], width)

    base = 7
    message = pl.pallas_call(
        functools.partial(product_kernel, (ways, depth, share, row_tiles, col_tiles), base),
        out_shape=jax.ShapeDtypeStruct((ways, depth * share + depth, width), jnp.float32),
        in_specs=[smem, vmem, vmem],
        out_specs=vmem,
        scratch_shapes=[pltpu.SMEM((row_tiles * col_tiles + 8,), jnp.int32)],
        compiler_params=pltpu.CompilerParams(vmem_limit_bytes=12 * 2**20),
    )(spots, tile_values, gathered)

    pairs = [[h * half + p * near + q for h in range(2) for q in range(near)] for p in range(depth)]
    came = lax.all_to_all(message.astype(jnp.float16), "col", 0, 0, axis_index_groups=pairs).astype(jnp.float32)
    spot = depth * share
    unit = (power(came[:, spot:], -1) * 2.0**-base)[:, :, None]
    blocks = jnp.sum(came[:, :spot].reshape(ways, depth, share, width) * unit, axis=0)

    rest = [[h * half + p * near + q for p in range(depth)] for h in range(2) for q in range(near)]
    message = (jnp.where(blocks < 0, -ROOT, ROOT) * jnp.sqrt(jnp.abs(blocks))).astype(jnp.float16)
    came = lax.all_to_all(message, "col", 0, 0, axis_index_groups=rest).astype(jnp.float32)
    summed = jnp.sum(came * jnp.abs(came), axis=0) * ROOT**-2

    output = jnp.dot(summed, weight.astype(jnp.float32), precision=lax.Precision.HIGHEST) + bias
    return jax.nn.relu(output).astype(jnp.bfloat16)


def solution(mesh):
    in_specs = (
        P(("col", "row"), None),
        P(),
        P(),
        P("row", "col", None, None, None),
        P("row", "col", None),
        P("row", "col", None),
        P("row", "col"),
    )
    out_specs = P(("row", "col"), None)
    return jax.shard_map(
        functools.partial(shards, mesh), mesh=mesh, in_specs=in_specs, out_specs=out_specs, check_vma=False
    )
```

```python
import functools

import jax
import jax.numpy as jnp
from jax import lax
from jax.experimental import pallas as pl
from jax.experimental.pallas import tpu as pltpu
from jax.sharding import PartitionSpec as P

LEVELS = 6
STEP = 16
ROOT = 1024.0


def level_of(peak, base):
    level = jnp.zeros(peak.shape, jnp.float32)
    for k in range(1, LEVELS + 1):
        level = level + jnp.where(peak < 2.0 ** (15 - base - STEP * k), 1.0, 0.0)
    return level


def power(level, sign):
    value = jnp.ones(level.shape, jnp.float32)
    for k in range(1, LEVELS + 1):
        value = value * jnp.where(level >= k, 2.0 ** (sign * STEP), 1.0)
    return value


def spread_kernel(features_ref, tiles_ref, spread_ref):
    for k in range(spread_ref.shape[0]):
        spread_ref[k] = features_ref[...]


def product_kernel(parts, base, spot_ref, tiles_ref, x_ref, out_ref, place_ref):
    ways, depth, share, row_tiles, col_tiles = parts
    _, _, slots, tile, _ = tiles_ref.shape
    near = ways // 2
    for p in range(row_tiles * col_tiles):
        place_ref[p] = slots
    for s in range(slots):
        place_ref[spot_ref[0, s]] = s

    def piece(p, lo, hi):
        slot = place_ref[p]
        rows = tiles_ref[0, 0, jnp.minimum(slot, slots - 1), lo:hi, :]
        return jnp.where(slot < slots, rows, jnp.zeros_like(rows))

    for d in range(ways * depth):
        way = (d // (near * depth)) * near + d % near
        at = (d % (near * depth)) // near
        value = jnp.zeros((share, x_ref.shape[1]), jnp.float32)
        for j in range(0, col_tiles, 2):
            strips = []
            row = d * share
            while row < (d + 1) * share:
                r, lo = row // tile, row % tile
                hi = min(tile, lo + (d + 1) * share - row)
                strips.append(
                    jnp.concatenate([piece(r * col_tiles + j + k, lo, hi) for k in range(2)], axis=1)
                )
                row += hi - lo
            value = value + jnp.dot(
                jnp.concatenate(strips, axis=0),
                x_ref[j * tile : (j + 2) * tile, :],
                preferred_element_type=jnp.float32,
            )
        level = level_of(jnp.max(jnp.abs(value), axis=0, keepdims=True), base)
        out_ref[way, at * share : (at + 1) * share, :] = value * (power(level, 1) * 2.0**base)
        out_ref[way, depth * share + at : depth * share + at + 1, :] = level


def shards(mesh, features, weight, bias, tile_values, tile_rows, tile_cols, tile_count):
    tile = tile_values.shape[3]
    width = features.shape[1]
    n_row, n_col = mesh.shape["row"], mesh.shape["col"]
    share = features.shape[0]
    total_rows = share * n_col
    half = n_col // 2
    near = 2
    ways = 2 * near
    depth = n_col // ways

    row_tiles, col_tiles = total_rows // tile, n_row * share // tile
    slots = tile_rows.shape[2]
    smem, vmem = pl.BlockSpec(memory_space=pltpu.SMEM), pl.BlockSpec(memory_space=pltpu.VMEM)
    spread = pl.pallas_call(
        spread_kernel,
        out_shape=jax.ShapeDtypeStruct((n_row,) + features.shape, features.dtype),
        in_specs=[vmem, pl.BlockSpec(memory_space=pltpu.HBM)],
        out_specs=vmem,
        compiler_params=pltpu.CompilerParams(vmem_limit_bytes=50 * 2**20),
    )(features, tile_values)
    used = (jnp.arange(slots, dtype=jnp.int32) < tile_count[0, 0]).astype(jnp.int32)
    spread, used = lax.optimization_barrier((spread, used))
    gathered = lax.all_to_all(spread, "row", 0, 0).reshape(n_row * features.shape[0], width)

    gathered, rows, cols = lax.optimization_barrier((gathered, tile_rows[0], tile_cols[0]))
    spots = jnp.where(used > 0, rows * col_tiles + cols, row_tiles * col_tiles)

    base = 7
    message = pl.pallas_call(
        functools.partial(product_kernel, (ways, depth, share, row_tiles, col_tiles), base),
        out_shape=jax.ShapeDtypeStruct((ways, depth * share + depth, width), jnp.float32),
        in_specs=[smem, vmem, vmem],
        out_specs=vmem,
        scratch_shapes=[pltpu.SMEM((row_tiles * col_tiles + 8,), jnp.int32)],
        compiler_params=pltpu.CompilerParams(vmem_limit_bytes=12 * 2**20),
    )(spots, tile_values, gathered)

    pairs = [[h * half + p * near + q for h in range(2) for q in range(near)] for p in range(depth)]
    came = lax.all_to_all(message.astype(jnp.float16), "col", 0, 0, axis_index_groups=pairs).astype(jnp.float32)
    spot = depth * share
    unit = (power(came[:, spot:], -1) * 2.0**-base)[:, :, None]
    blocks = jnp.sum(came[:, :spot].reshape(ways, depth, share, width) * unit, axis=0)

    rest = [[h * half + p * near + q for p in range(depth)] for h in range(2) for q in range(near)]
    message = (jnp.where(blocks < 0, -ROOT, ROOT) * jnp.sqrt(jnp.abs(blocks))).astype(jnp.float16)
    came = lax.all_to_all(message, "col", 0, 0, axis_index_groups=rest).astype(jnp.float32)
    summed = jnp.sum(came * jnp.abs(came), axis=0) * ROOT**-2

    output = jnp.dot(summed, weight.astype(jnp.float32), precision=lax.Precision.HIGHEST) + bias
    return jax.nn.relu(output).astype(jnp.bfloat16)


def solution(mesh):
    in_specs = (
        P(("col", "row"), None),
        P(),
        P(),
        P("row", "col", None, None, None),
        P("row", "col", None),
        P("row", "col", None),
        P("row", "col"),
    )
    out_specs = P(("row", "col"), None)
    return jax.shard_map(
        functools.partial(shards, mesh), mesh=mesh, in_specs=in_specs, out_specs=out_specs, check_vma=False
    )
```

```python
import functools

import jax
import jax.numpy as jnp
from jax import lax
from jax.experimental import pallas as pl
from jax.experimental.pallas import tpu as pltpu
from jax.sharding import PartitionSpec as P

LEVELS = 6
STEP = 16
ROOT = 1024.0


def level_of(peak, base):
    level = jnp.zeros(peak.shape, jnp.float32)
    for k in range(1, LEVELS + 1):
        level = level + jnp.where(peak < 2.0 ** (15 - base - STEP * k), 1.0, 0.0)
    return level


def power(level, sign):
    value = jnp.ones(level.shape, jnp.float32)
    for k in range(1, LEVELS + 1):
        value = value * jnp.where(level >= k, 2.0 ** (sign * STEP), 1.0)
    return value


def spread_kernel(features_ref, tiles_ref, spread_ref):
    for k in range(spread_ref.shape[0]):
        spread_ref[k] = features_ref[...]


def product_kernel(parts, base, place_ref, tiles_ref, x_ref, out_ref):
    ways, depth, share, row_tiles, col_tiles = parts
    _, _, slots, tile, _ = tiles_ref.shape
    near = ways // 2
    def piece(p, lo, hi):
        slot = place_ref[p]
        rows = tiles_ref[0, 0, jnp.minimum(slot, slots - 1), lo:hi, :]
        return jnp.where(slot < slots, rows, jnp.zeros_like(rows))

    for d in range(ways * depth):
        way = (d // (near * depth)) * near + d % near
        at = (d % (near * depth)) // near
        value = jnp.zeros((share, x_ref.shape[1]), jnp.float32)
        for j in range(0, col_tiles, 2):
            strips = []
            row = d * share
            while row < (d + 1) * share:
                r, lo = row // tile, row % tile
                hi = min(tile, lo + (d + 1) * share - row)
                strips.append(
                    jnp.concatenate([piece(r * col_tiles + j + k, lo, hi) for k in range(2)], axis=1)
                )
                row += hi - lo
            value = value + jnp.dot(
                jnp.concatenate(strips, axis=0),
                x_ref[j * tile : (j + 2) * tile, :],
                preferred_element_type=jnp.float32,
            )
        level = level_of(jnp.max(jnp.abs(value), axis=0, keepdims=True), base)
        out_ref[way, at * share : (at + 1) * share, :] = value * (power(level, 1) * 2.0**base)
        out_ref[way, depth * share + at : depth * share + at + 1, :] = level


def shards(mesh, features, weight, bias, tile_values, tile_rows, tile_cols, tile_count):
    tile = tile_values.shape[3]
    width = features.shape[1]
    n_row, n_col = mesh.shape["row"], mesh.shape["col"]
    share = features.shape[0]
    total_rows = share * n_col
    half = n_col // 2
    near = 2
    ways = 2 * near
    depth = n_col // ways

    row_tiles, col_tiles = total_rows // tile, n_row * share // tile
    slots = tile_rows.shape[2]
    smem, vmem = pl.BlockSpec(memory_space=pltpu.SMEM), pl.BlockSpec(memory_space=pltpu.VMEM)
    spread = pl.pallas_call(
        spread_kernel,
        out_shape=jax.ShapeDtypeStruct((n_row,) + features.shape, features.dtype),
        in_specs=[vmem, pl.BlockSpec(memory_space=pltpu.HBM)],
        out_specs=vmem,
        compiler_params=pltpu.CompilerParams(vmem_limit_bytes=50 * 2**20),
    )(features, tile_values)
    index = jnp.arange(slots, dtype=jnp.int32)
    used = jnp.where(index < tile_count[0, 0], index - slots, 0)
    spread, used = lax.optimization_barrier((spread, used))
    gathered = lax.all_to_all(spread, "row", 0, 0).reshape(n_row * features.shape[0], width)

    gathered, rows, cols = lax.optimization_barrier((gathered, tile_rows[0], tile_cols[0]))
    spots = rows * col_tiles + cols

    here = spots[0][None, :] == jnp.arange(row_tiles * col_tiles, dtype=jnp.int32)[:, None]
    place = slots + jnp.sum(jnp.where(here, used, 0), axis=1)

    base = 7
    message = pl.pallas_call(
        functools.partial(product_kernel, (ways, depth, share, row_tiles, col_tiles), base),
        out_shape=jax.ShapeDtypeStruct((ways, depth * share + depth, width), jnp.float32),
        in_specs=[smem, vmem, vmem],
        out_specs=vmem,
        compiler_params=pltpu.CompilerParams(vmem_limit_bytes=12 * 2**20),
    )(place, tile_values, gathered)

    pairs = [[h * half + p * near + q for h in range(2) for q in range(near)] for p in range(depth)]
    came = lax.all_to_all(message.astype(jnp.float16), "col", 0, 0, axis_index_groups=pairs).astype(jnp.float32)
    spot = depth * share
    unit = (power(came[:, spot:], -1) * 2.0**-base)[:, :, None]
    blocks = jnp.sum(came[:, :spot].reshape(ways, depth, share, width) * unit, axis=0)

    rest = [[h * half + p * near + q for p in range(depth)] for h in range(2) for q in range(near)]
    message = (jnp.where(blocks < 0, -ROOT, ROOT) * jnp.sqrt(jnp.abs(blocks))).astype(jnp.float16)
    came = lax.all_to_all(message, "col", 0, 0, axis_index_groups=rest).astype(jnp.float32)
    summed = jnp.sum(came * jnp.abs(came), axis=0) * ROOT**-2

    output = jnp.dot(summed, weight.astype(jnp.float32), precision=lax.Precision.HIGHEST) + bias
    return jax.nn.relu(output).astype(jnp.bfloat16)


def solution(mesh):
    in_specs = (
        P(("col", "row"), None),
        P(),
        P(),
        P("row", "col", None, None, None),
        P("row", "col", None),
        P("row", "col", None),
        P("row", "col"),
    )
    out_specs = P(("row", "col"), None)
    return jax.shard_map(
        functools.partial(shards, mesh), mesh=mesh, in_specs=in_specs, out_specs=out_specs, check_vma=False
    )
```

```python
import functools

import jax
import jax.numpy as jnp
from jax import lax
from jax.experimental import pallas as pl
from jax.experimental.pallas import tpu as pltpu
from jax.sharding import PartitionSpec as P

LEVELS = 6
STEP = 16
ROOT = 1024.0


def level_of(peak, base):
    level = jnp.zeros(peak.shape, jnp.float32)
    scale = jnp.ones(peak.shape, jnp.float32)
    for k in range(1, LEVELS + 1):
        small = peak < 2.0 ** (15 - base - STEP * k)
        level = jnp.where(small, float(k), level)
        scale = jnp.where(small, 2.0 ** (STEP * k), scale)
    return level, scale


def power(level, sign):
    value = jnp.ones(level.shape, jnp.float32)
    for k in range(1, LEVELS + 1):
        value = value * jnp.where(level >= k, 2.0 ** (sign * STEP), 1.0)
    return value


def spread_kernel(features_ref, tiles_ref, spread_ref):
    for k in range(spread_ref.shape[0]):
        spread_ref[k] = features_ref[...]


def product_kernel(parts, base, place_ref, tiles_ref, x_ref, out_ref):
    ways, depth, share, row_tiles, col_tiles = parts
    _, _, slots, tile, _ = tiles_ref.shape
    near = ways // 2
    def piece(p, lo, hi):
        slot = place_ref[p]
        rows = tiles_ref[0, 0, jnp.minimum(slot, slots - 1), lo:hi, :]
        return jnp.where(slot < slots, rows, jnp.zeros_like(rows))

    for d in range(ways * depth):
        way = (d // (near * depth)) * near + d % near
        at = (d % (near * depth)) // near
        value = jnp.zeros((share, x_ref.shape[1]), jnp.float32)
        for j in range(0, col_tiles, 2):
            strips = []
            row = d * share
            while row < (d + 1) * share:
                r, lo = row // tile, row % tile
                hi = min(tile, lo + (d + 1) * share - row)
                strips.append(
                    jnp.concatenate([piece(r * col_tiles + j + k, lo, hi) for k in range(2)], axis=1)
                )
                row += hi - lo
            value = value + jnp.dot(
                jnp.concatenate(strips, axis=0),
                x_ref[j * tile : (j + 2) * tile, :],
                preferred_element_type=jnp.float32,
            )
        level, scale = level_of(jnp.max(jnp.abs(value), axis=0, keepdims=True), base)
        out_ref[way, at * share : (at + 1) * share, :] = value * (scale * 2.0**base)
        out_ref[way, depth * share + at : depth * share + at + 1, :] = level


def shards(mesh, features, weight, bias, tile_values, tile_rows, tile_cols, tile_count):
    tile = tile_values.shape[3]
    width = features.shape[1]
    n_row, n_col = mesh.shape["row"], mesh.shape["col"]
    share = features.shape[0]
    total_rows = share * n_col
    half = n_col // 2
    near = 2
    ways = 2 * near
    depth = n_col // ways

    row_tiles, col_tiles = total_rows // tile, n_row * share // tile
    slots = tile_rows.shape[2]
    smem, vmem = pl.BlockSpec(memory_space=pltpu.SMEM), pl.BlockSpec(memory_space=pltpu.VMEM)
    spread = pl.pallas_call(
        spread_kernel,
        out_shape=jax.ShapeDtypeStruct((n_row,) + features.shape, features.dtype),
        in_specs=[vmem, pl.BlockSpec(memory_space=pltpu.HBM)],
        out_specs=vmem,
        compiler_params=pltpu.CompilerParams(vmem_limit_bytes=50 * 2**20),
    )(features, tile_values)
    index = jnp.arange(slots, dtype=jnp.int32)
    used = jnp.where(index < tile_count[0, 0], index - slots, 0)
    spread, used = lax.optimization_barrier((spread, used))
    gathered = lax.all_to_all(spread, "row", 0, 0).reshape(n_row * features.shape[0], width)

    gathered, rows, cols = lax.optimization_barrier((gathered, tile_rows[0], tile_cols[0]))
    spots = rows * col_tiles + cols

    here = spots[0][None, :] == jnp.arange(row_tiles * col_tiles, dtype=jnp.int32)[:, None]
    place = slots + jnp.sum(jnp.where(here, used, 0), axis=1)

    base = 7
    message = pl.pallas_call(
        functools.partial(product_kernel, (ways, depth, share, row_tiles, col_tiles), base),
        out_shape=jax.ShapeDtypeStruct((ways, depth * share + depth, width), jnp.float32),
        in_specs=[smem, vmem, vmem],
        out_specs=vmem,
        compiler_params=pltpu.CompilerParams(vmem_limit_bytes=12 * 2**20),
    )(place, tile_values, gathered)

    pairs = [[h * half + p * near + q for h in range(2) for q in range(near)] for p in range(depth)]
    came = lax.all_to_all(message.astype(jnp.float16), "col", 0, 0, axis_index_groups=pairs).astype(jnp.float32)
    spot = depth * share
    unit = (power(came[:, spot:], -1) * 2.0**-base)[:, :, None]
    blocks = jnp.sum(came[:, :spot].reshape(ways, depth, share, width) * unit, axis=0)

    rest = [[h * half + p * near + q for p in range(depth)] for h in range(2) for q in range(near)]
    message = (jnp.where(blocks < 0, -ROOT, ROOT) * jnp.sqrt(jnp.abs(blocks))).astype(jnp.float16)
    came = lax.all_to_all(message, "col", 0, 0, axis_index_groups=rest).astype(jnp.float32)
    summed = jnp.sum(came * jnp.abs(came), axis=0) * ROOT**-2

    output = jnp.dot(summed, weight.astype(jnp.float32), precision=lax.Precision.HIGHEST) + bias
    return jax.nn.relu(output).astype(jnp.bfloat16)


def solution(mesh):
    in_specs = (
        P(("col", "row"), None),
        P(),
        P(),
        P("row", "col", None, None, None),
        P("row", "col", None),
        P("row", "col", None),
        P("row", "col"),
    )
    out_specs = P(("row", "col"), None)
    return jax.shard_map(
        functools.partial(shards, mesh), mesh=mesh, in_specs=in_specs, out_specs=out_specs, check_vma=False
    )
```
